512 devices in a mesh: dp: 16 (over x, z_lo), ctx: 32 (over z_hi, y, core).
Axes of the slice: x: 4, y: 4, z: 16 (z_hi: 4, z_lo: 4; z = z_hi * 4 + z_lo), core: 2. Of those that a mesh axis runs over, the one named last changes fastest.
Arguments:
- query_rows: bfloat16 [65536, 512], P(('dp', 'ctx')), may hold values from -6 to 6
- key_rows: bfloat16 [65536, 512], P(('dp', 'ctx')), may hold values from -6 to 6
- value_rows: bfloat16 [65536, 512], P(('dp', 'ctx')), may hold values from -6 to 6
- gate_rows: bfloat16 [65536, 512], P(('dp', 'ctx')), may hold values from -6 to 6
- positives: bfloat16 [65536, 512], P(('dp', 'ctx')), may hold values from -0.8984375 to 0.8984375
- negatives: bfloat16 [512, 512], P('dp'), may hold values from -18 to 18
- history_lengths: int32 [16, 4], P('dp'), may hold values from 1 to 2048, 4096 in all within a row
Outputs:
- grad_queries: bfloat16 [65536, 512], P(('dp', 'ctx'))
- grad_gates: bfloat16 [65536, 512], P(('dp', 'ctx'))
- grad_negatives: float32 [512, 512], P(('dp', 'ctx'))
The draws below stay inside these ranges and needn't reach their ends.
Inputs may be any that keep to these rules, and one draw needn't show every extreme that they name: `history_lengths`: each row sums to 4096; its longest history is exactly 2048.
All inputs are finite; a program needn't handle non-finite values.
Results may differ from the reference program's by a relative error of at most 0.022.
The reference program's roundings to bfloat16 on the way count: a program that leaves them out, or rounds other values in their place, can miss the bound.
Values may be sent and summed in bfloat16 or wider, within the bound.
A program may use at most 64 MiB of HBM per device.

```python
import math
import jax
import jax.numpy as jnp
import numpy as np
from jax import lax

HEADS = 4
WIDTH = 512
USERS = 4
EVENTS = 4096
TOKENS = 65536
NEG = 512
N_DP = 16


def draw_negatives(key, part):
    key = jax.random.fold_in(key, 11)
    base_key = jax.random.fold_in(key, 0)
    values = jnp.clip(jax.random.normal(base_key, (NEG, WIDTH), jnp.float32), -6.0, 6.0) * 0.15
    return values.astype(jnp.bfloat16)


def steps_of(own_key, shape, cuts, least, high):
    level = 1.0
    for axis_at, blocks in cuts:
        heights = jax.random.uniform(jax.random.fold_in(jax.random.fold_in(own_key, 6), axis_at), (blocks,), jnp.float32, least / len(cuts), high / len(cuts))
        level = level * jnp.repeat(jnp.exp(heights), shape[axis_at] // blocks).reshape((-1,) + (1,) * (len(shape) - 1 - axis_at))
    return level


def length_profile(amount, total, bound, skew):
    loads = [(1 << 20) // math.isqrt(grade ** skew) + 1 for grade in range(2, amount + 1)]
    rest, counts = total - bound - (amount - 1), [1] * (amount - 1)
    while rest > 0:
        free = [i for i in range(amount - 1) if counts[i] < bound]
        whole, left = sum([loads[i] for i in free]), rest
        for i in free:
            extra = min(bound - counts[i], max(1, left * loads[i] // whole), rest)
            counts[i] = counts[i] + extra
            rest = rest - extra
    return np.array([bound] + counts)


def uneven_parts(rng, count, total, limit, lean):
    if count == 2:
        one = jax.random.randint(rng, (), max(1, total - limit), min(limit, total - 1) + 1)
        return jnp.stack([one, total - one])
    sizes = jnp.asarray(length_profile(count, total, limit, lean), jnp.int32)
    pairs = (count - 1) // 2
    giver, receiver = sizes[1:1 + 2 * pairs:2], sizes[2:2 + 2 * pairs:2]
    slack = jnp.minimum(giver - 1, limit - receiver)
    shifted = jax.random.randint(jax.random.fold_in(rng, 1), (pairs,), 0, 1 << 20) % (slack + 1)
    sizes = sizes.at[1:1 + 2 * pairs:2].set(giver - shifted).at[2:2 + 2 * pairs:2].set(receiver + shifted)
    return sizes[jax.random.permutation(jax.random.fold_in(rng, 2), count)]


def gaussian(key, extent, spread, most, cuts=(), kind=jnp.bfloat16):
    drawn = jax.random.normal(key, extent, jnp.float32) * spread
    if len(cuts) > 0:
        drawn = steps_of(key, extent, cuts, -0.22, 0.18) * drawn
    return jnp.clip(drawn, min=-most, max=most).astype(kind)


def setup_inputs(seed: int = 0) -> dict:
    arg_keys = jax.random.split(jax.random.key(seed), 8)
    query_rows = gaussian(arg_keys[0], (TOKENS, WIDTH), 1.0, 6.0, ((0, 512),))
    key_rows = gaussian(arg_keys[1], (TOKENS, WIDTH), 1.0, 6.0, ((0, 512),))
    value_rows = gaussian(arg_keys[2], (TOKENS, WIDTH), 1.0, 6.0, ((0, 512),))
    gate_rows = gaussian(arg_keys[3], (TOKENS, WIDTH), 1.0, 6.0, ((0, 512),))
    positives = gaussian(arg_keys[4], (TOKENS, WIDTH), 0.15, 0.8984375, ((0, 512),))
    negatives = draw_negatives(jax.random.fold_in(arg_keys[7], 71), 0)
    history_lengths = jax.vmap(lambda own: uneven_parts(own, USERS, EVENTS, EVENTS // 2, 2))(jax.random.split(arg_keys[6], N_DP)).reshape((N_DP, USERS)).astype(jnp.int32)
    return dict(query_rows=query_rows, key_rows=key_rows, value_rows=value_rows, gate_rows=gate_rows, positives=positives, negatives=negatives, history_lengths=history_lengths)


eps = 1e-05

def segment_of(places, bounds):
    return lax.optimization_barrier(jnp.sum((places[:, None] >= bounds[None, :]).astype(jnp.int32), axis=1))

def rounded(values):
    return lax.optimization_barrier(values.astype(jnp.bfloat16)).astype(jnp.float32)

def group_pass(group_arrays, negatives):
    q_group, k_group, v_group, g_group, p_group, group_lengths = group_arrays
    event_count, feature_count = q_group.shape
    head_size = feature_count // HEADS
    score_scale = head_size ** (-0.5)
    user_ends = jnp.cumsum(group_lengths).astype(jnp.int32)
    places = jnp.arange(event_count, dtype=jnp.int32)
    user_ids = segment_of(places, user_ends)
    q_heads = q_group.astype(jnp.float32).reshape(event_count, HEADS, head_size)
    k_heads = k_group.astype(jnp.float32).reshape(event_count, HEADS, head_size)
    v_heads = v_group.astype(jnp.float32).reshape(event_count, HEADS, head_size)
    block_rows = math.gcd(event_count, 512)
    offsets = jnp.arange(event_count // block_rows, dtype=jnp.int32) * block_rows

    def scores(offset):
        q_block = lax.dynamic_slice_in_dim(q_heads, offset, block_rows, 0)
        row_places = offset + jnp.arange(block_rows, dtype=jnp.int32)
        row_users = lax.dynamic_slice_in_dim(user_ids, offset, block_rows, 0)
        allowed = (row_users[:, None] == user_ids[None, :]) & (places[None, :] <= row_places[:, None])
        logits = jnp.einsum('rhd,khd->hrk', q_block, k_heads) * score_scale
        return (logits, allowed[None])

    def forward(offset):
        logits, allowed = scores(offset)
        weights = rounded(jnp.where(allowed, jax.nn.silu(logits), 0.0))
        return jnp.einsum('hrk,khd->rhd', weights, v_heads)
    attended = lax.map(forward, offsets).reshape(event_count, feature_count)
    inverse_rms = lax.rsqrt(lax.optimization_barrier(jnp.mean(attended * attended, axis=1, keepdims=True)) + eps)
    normed = attended * inverse_rms
    gates_wide = g_group.astype(jnp.float32)
    positive_wide = p_group.astype(jnp.float32)
    hidden_b = (normed * gates_wide).astype(jnp.bfloat16)
    own_logit = lax.optimization_barrier(jnp.sum(hidden_b.astype(jnp.float32) * positive_wide, axis=1))
    other_logits = jnp.dot(hidden_b, negatives.T, preferred_element_type=jnp.float32)
    largest = jnp.maximum(own_logit, lax.optimization_barrier(jnp.max(other_logits, axis=1)))
    exp_own = jnp.exp(own_logit - largest)
    exp_others = jnp.exp(other_logits - largest[:, None])
    partition = exp_own + lax.optimization_barrier(jnp.sum(exp_others, axis=1))
    probs_b = (exp_others / partition[:, None]).astype(jnp.bfloat16)
    own_prob = exp_own / partition
    d_hidden = (own_prob - 1.0)[:, None] * positive_wide + jnp.dot(probs_b, negatives, preferred_element_type=jnp.float32)
    grad_gates = (d_hidden * normed).astype(jnp.bfloat16)
    d_normed = d_hidden * gates_wide
    d_attended = inverse_rms * (d_normed - normed * lax.optimization_barrier(jnp.mean(d_normed * normed, axis=1, keepdims=True)))
    d_heads = rounded(d_attended).reshape(event_count, HEADS, head_size)

    def backward(offset):
        logits, allowed = scores(offset)
        d_block = lax.dynamic_slice_in_dim(d_heads, offset, block_rows, 0)
        d_weights = jnp.einsum('rhd,khd->hrk', d_block, v_heads)
        sigmoid_values = jax.nn.sigmoid(logits)
        d_logits = rounded(jnp.where(allowed, d_weights * sigmoid_values * (1.0 + logits * (1.0 - sigmoid_values)) * score_scale, 0.0))
        return jnp.einsum('hrk,khd->rhd', d_logits, k_heads)
    grad_queries = lax.map(backward, offsets).reshape(event_count, feature_count).astype(jnp.bfloat16)
    neg_term = jnp.dot(probs_b.T, hidden_b, preferred_element_type=jnp.float32)
    return (grad_queries, grad_gates, neg_term)

def reference(query_rows, key_rows, value_rows, gate_rows, positives, negatives, history_lengths):
    feature_count = query_rows.shape[1]

    def by_group(array):
        return array.reshape(N_DP, array.shape[0] // N_DP, feature_count)

    def one_group(group_arrays):
        return group_pass(group_arrays, negatives)
    group_arrays = (by_group(query_rows), by_group(key_rows), by_group(value_rows), by_group(gate_rows), by_group(positives), history_lengths)
    grad_queries, grad_gates, neg_terms = lax.map(one_group, group_arrays)
    grad_negatives = lax.optimization_barrier(jnp.sum(neg_terms, axis=0))
    return (grad_queries.reshape(-1, feature_count), grad_gates.reshape(-1, feature_count), grad_negatives)
```

```python
import jax
import jax.numpy as jnp
from jax import lax
from jax.experimental import pallas as pl
from jax.experimental.pallas import tpu as pltpu
from jax.sharding import PartitionSpec as P

HEADS = 4
HEAD = 128
WIDTH = 512
ROWS = 128
QUARTER = 32
SCALE = HEAD ** (-0.5)
EPS = 1e-05
MESH = pl.DeviceIdType.MESH

ORDER_1 = (0, 1, 2, 3)
ORDER_2 = (0, 2, 6, 4, 7, 5, 1, 3)
ORDER_3 = (0, 1, 4, 5, 2, 6, 3, 7)


def packed(order):
    return sum(code << (3 * place) for place, code in enumerate(order))


def pick(h, values):
    out = jnp.int32(values[3])
    for index in (2, 1, 0):
        out = jnp.where(h == index, jnp.int32(values[index]), out)
    return out


def dot_last(a, b):
    return lax.dot_general(a, b, (((1,), (1,)), ((), ())), preferred_element_type=jnp.float32)


def dot_first(a, b):
    return lax.dot_general(a, b, (((0,), (0,)), ((), ())), preferred_element_type=jnp.float32)


def dot(a, b):
    return jnp.dot(a, b, preferred_element_type=jnp.float32)


def kernel(
    lengths, q_ref, k_hbm, v_hbm, gate_ref, pos_ref, neg_ref,
    gq_out, gg_out, gn_out,
    kv, att, slope, negs_raw, negs, d_att, c_send, c_recv, own_half, xy_send, xy_recv, z_send, z_recv,
    local_sem, kv_recv, z_sem, y_sem, c_sem,
    nx_send, nx_recv, nl_send, nl_recv, ny_send, ny_recv, nc_send, nc_recv,
    rc_send, rc_recv, rxy_send, rxy_recv, rz_send, rz_recv,
):
    dp, ctx = lax.axis_index("dp"), lax.axis_index("ctx")
    x, l = dp // 4, dp % 4
    h, y, c = ctx // 8, (ctx // 2) % 4, ctx % 2
    z = h * 4 + l

    def device(x2, l2, h2, y2, c2):
        return (x2 * 4 + l2, (h2 * 4 + y2) * 2 + c2)

    sibling = device(x, l, h, y, 1 - c)

    def z_peer(k):
        z2 = (z + k) % 16
        return z2, device(x, z2 % 4, z2 // 4, y, c)

    def xy_peer(k):
        x2, y2 = (x + k // 4) % 4, (y + k % 4) % 4
        return x2 * 4 + y2, device(x2, l, h, y2, c)

    local = []
    for q in range(4):
        for kind, source in ((0, k_hbm), (1, v_hbm)):
            local.append(pltpu.make_async_copy(
                source.at[pl.ds(q * QUARTER, QUARTER)], kv.at[h, q, kind, y, c], local_sem.at[q * 2 + kind]))
    for copy in local:
        copy.start()

    barrier = pltpu.get_barrier_semaphore()
    pl.semaphore_signal(barrier, inc=1, device_id=sibling, device_id_type=MESH)
    for k in range(1, 16):
        pl.semaphore_signal(barrier, inc=1, device_id=z_peer(k)[1], device_id_type=MESH)
        pl.semaphore_signal(barrier, inc=1, device_id=xy_peer(k)[1], device_id_type=MESH)

    for y2 in range(4):
        @pl.when(y2 > y)
        def _():
            for q in range(4):
                kv[h, q, :, y2] = jnp.zeros((2, 2, QUARTER, WIDTH), jnp.bfloat16)

        @pl.when((h >= 2) & (y2 < y))
        def _():
            for q in range(4):
                kv[h - 2, q, :, y2] = jnp.zeros((2, 2, QUARTER, WIDTH), jnp.bfloat16)

    att[...] = jnp.zeros_like(att)
    for copy in local:
        copy.wait()
    pl.semaphore_wait(barrier, 31)

    def piece_copy(hb, q, y2, c2, send_sem, target):
        piece = kv.at[hb, q, :, y2, c2]
        return pltpu.make_async_remote_copy(
            src_ref=piece, dst_ref=piece, send_sem=send_sem, recv_sem=kv_recv.at[hb, q, y2, c2],
            device_id=target, device_id_type=MESH)

    def piece_arrived(hb, q, y2, c2):
        piece_copy(hb, q, y2, c2, z_sem.at[0, 0, 0], sibling).wait_recv()

    def forward(hb, q, kind):
        return piece_copy(hb, q, y, c, z_sem.at[0, kind, q], device(x, l, (h + 1) % 4, y, c))

    def backward(hb, q, kind):
        return piece_copy(hb, q, y, c, z_sem.at[1, kind, q], device(x, l, (h + 3) % 4, y, c))

    def sends_forward(q):
        return (h <= 2) if q != 1 else ((h == 0) | (h == 2))

    def sends_backward(q):
        return {0: h < 0, 1: h == 1, 2: h <= 1, 3: h <= 1}[q]

    for q in range(4):
        pl.when(sends_forward(q))(lambda q=q: forward(h, q, 0).start())
        if q > 0:
            pl.when(sends_backward(q))(lambda q=q: backward(h, q, 0).start())

    def neg_x(k):
        part = neg_ref.at[pl.ds(c * 16, 16)]
        return pltpu.make_async_remote_copy(
            src_ref=part, dst_ref=negs_raw.at[y, c, l], send_sem=nx_send.at[k - 1], recv_sem=nx_recv.at[0],
            device_id=device((x + k) % 4, l, h, y, c), device_id_type=MESH)

    def neg_z(k):
        part = negs_raw.at[y, c, l]
        l2 = (l + k) % 4
        z2 = (z + (k if k < 3 else 15)) % 16
        return pltpu.make_async_remote_copy(
            src_ref=part, dst_ref=part, send_sem=nl_send.at[k - 1], recv_sem=nl_recv.at[k - 1],
            device_id=device(x, l2, z2 // 4, y, c), device_id_type=MESH)

    def neg_z_arrived(k):
        part = negs_raw.at[y, c, (l + 4 - k) % 4]
        pltpu.make_async_remote_copy(
            src_ref=part, dst_ref=part, send_sem=nl_send.at[k - 1], recv_sem=nl_recv.at[k - 1],
            device_id=sibling, device_id_type=MESH).wait_recv()

    def neg_y(k):
        part = negs_raw.at[y, c]
        return pltpu.make_async_remote_copy(
            src_ref=part, dst_ref=part, send_sem=ny_send.at[k - 1], recv_sem=ny_recv.at[k - 1],
            device_id=device(x, l, h, (y + k) % 4, c), device_id_type=MESH)

    def neg_y_arrived(k):
        part = negs_raw.at[(y + 4 - k) % 4, c]
        pltpu.make_async_remote_copy(
            src_ref=part, dst_ref=part, send_sem=ny_send.at[k - 1], recv_sem=ny_recv.at[k - 1],
            device_id=sibling, device_id_type=MESH).wait_recv()

    def neg_c(c2):
        part = negs_raw.at[:, c2]
        return pltpu.make_async_remote_copy(
            src_ref=part, dst_ref=part, send_sem=nc_send.at[0], recv_sem=nc_recv.at[0],
            device_id=sibling, device_id_type=MESH)

    @pl.when(x == y)
    def _():
        for k in (1, 2, 3):
            neg_x(k).start()

    places = ctx * ROWS + lax.broadcasted_iota(jnp.int32, (ROWS, 1), 0)
    first = jnp.zeros((ROWS, 1), jnp.int32)
    user_end = jnp.int32(0)
    for user in range(4):
        user_end = user_end + lengths[0, user]
        first = jnp.where(places >= user_end, user_end, first)

    orders = pick(h, [0, packed(ORDER_1), packed(ORDER_2), packed(ORDER_3)])
    ranks = pick(h, [4, 8, 12, 12])

    def rank_of(e):
        code = lax.shift_right_logical(orders, 3 * jnp.maximum(e - 4, 0)) & 7
        back = jnp.where(e < 4, 0, 1 + code // 4)
        return back, jnp.where(e < 4, e, code % 4)

    def comes_from(back, y2):
        return (back == 1) | ((back == 0) & (y2 < y)) | ((back == 2) & (y2 > y))

    def goes_to(back, y2):
        return (back == 1) | ((back == 0) & (y2 > y)) | ((back == 2) & (y2 < y))

    def z_forwards(back, q):
        return ((h == 1) & (back == 1) & (q < 2)) | ((h == 2) & (back == 1) & (q == 0))

    def z_backwards(back, q):
        return (h == 3) & (back == 2) & (q == 1)

    def y_copy(e, hb, q, k):
        return piece_copy(hb, q, y, c, y_sem.at[e, k - 1], device(x, l, h, (y + k) % 4, c))

    def c_copy(e, hb, q, y2):
        return piece_copy(hb, q, y2, c, c_sem.at[e, y2], sibling)

    def transit(hb, q):
        piece_arrived(hb, q, y, c)
        backward(hb, q, 1).start()

    def column_event(e):
        back, q = rank_of(e)
        hb = h - back
        pl.when(back > 0)(lambda: piece_arrived(hb, q, y, c))
        pl.when(z_forwards(back, q))(lambda: forward(hb, q, 1).start())
        pl.when(z_backwards(back, q))(lambda: backward(hb, q, 1).start())
        for k in (1, 3, 2):
            pl.when(goes_to(back, (y + k) % 4))(lambda k=k: y_copy(e, hb, q, k).start())
        c_copy(e, hb, q, y).start()

    def row_event(e):
        back, q = rank_of(e)
        hb = h - back
        for k in (1, 3, 2):
            y2 = (y + k) % 4

            @pl.when(comes_from(back, y2))
            def _():
                piece_arrived(hb, q, y2, c)
                c_copy(e, hb, q, y2).start()

    def compute_event(e):
        back, q = rank_of(e)
        hb = h - back
        for k in range(4):
            y2 = (y + k) % 4
            pl.when(True if k == 0 else comes_from(back, y2))(lambda y2=y2: piece_arrived(hb, q, y2, 1 - c))
        at = lax.broadcasted_iota(jnp.int32, (ROWS, 8 * QUARTER), 1)
        k_places = hb * 1024 + q * QUARTER + (at // QUARTER) * ROWS + at % QUARTER
        allowed = (k_places >= first) & (k_places <= places)
        for head in range(HEADS):
            lanes = pl.ds(head * HEAD, HEAD)
            k_head = kv[hb, q, 0, :, :, :, lanes].reshape(8 * QUARTER, HEAD)
            v_head = kv[hb, q, 1, :, :, :, lanes].reshape(8 * QUARTER, HEAD)
            logits = dot_last(q_ref[:, lanes], k_head)
            sigmoid = 0.5 * jnp.tanh(logits * (0.5 * SCALE)) + 0.5
            silu = logits * SCALE * sigmoid
            weights = jnp.where(allowed, silu, 0.0).astype(jnp.bfloat16)
            slope[e, head] = jnp.where(allowed, (sigmoid + silu * (1.0 - sigmoid)) * SCALE, 0.0)
            att[:, lanes] += dot(weights, v_head)

    def step(e, carry):
        pl.when(e < ranks)(lambda: column_event(e))

        @pl.when(h == 3)
        def _():
            pl.when(e == 4)(lambda: transit(0, 2))
            pl.when(e == 5)(lambda: transit(0, 3))

        @pl.when(e == 2)
        def _():
            @pl.when(x != y)
            def _():
                part = negs_raw.at[y, c, l]
                pltpu.make_async_remote_copy(
                    src_ref=part, dst_ref=part, send_sem=nx_send.at[0], recv_sem=nx_recv.at[0],
                    device_id=sibling, device_id_type=MESH).wait_recv()

            @pl.when(x == y)
            def _():
                negs_raw[y, c, l] = neg_ref[pl.ds(pl.multiple_of(c * 16, 16), 16), :]

            for k in (1, 2, 3):
                neg_z(k).start()

        @pl.when(e == 4)
        def _():
            for k in (1, 2, 3):
                neg_z_arrived(k)
            for k in (1, 2, 3):
                neg_y(k).start()

        @pl.when(e == 5)
        def _():
            for k in (1, 2, 3):
                neg_y_arrived(k)
            neg_c(c).start()

        pl.when(e >= 2)(lambda: compute_event(e - 2))
        pl.when((e >= 1) & (e <= ranks))(lambda: row_event(e - 1))
        return carry

    @pl.when(h == 0)
    def _():
        lax.fori_loop(0, 6, step, 0)
        for q in (1, 2, 3):
            transit(1, q)

    @pl.when(h != 0)
    def _():
        lax.fori_loop(0, ranks + 2, step, 0)

    neg_c(1 - c).wait_recv()
    to = lax.broadcasted_iota(jnp.int32, (512, 512), 0)
    source = ((((to // 64) % 4 * 2 + (to // 8) % 2) * 4 + to % 4) * 16
              + (to // 4) % 2 * 8 + (to // 16) % 4 * 2 + to // 256)
    chosen = lax.broadcasted_iota(jnp.int32, (512, 512), 1) == source
    negs[...] = dot(
        jnp.where(chosen, 1.0, 0.0).astype(jnp.bfloat16), negs_raw[...].reshape(512, WIDTH)
    ).astype(jnp.bfloat16)

    attended = att[...]
    inverse_rms = lax.rsqrt(jnp.mean(attended * attended, axis=1, keepdims=True) + EPS)
    normed = attended * inverse_rms
    gates = gate_ref[...].astype(jnp.float32)
    positives = pos_ref[...].astype(jnp.float32)
    hidden = (normed * gates).astype(jnp.bfloat16)
    own_logit = jnp.sum(hidden.astype(jnp.float32) * positives, axis=1, keepdims=True)
    other_logits = dot_last(hidden, negs[...])
    largest = jnp.maximum(own_logit, jnp.max(other_logits, axis=1, keepdims=True))
    exp_own = jnp.exp(own_logit - largest)
    exp_others = jnp.exp(other_logits - largest)
    partition = exp_own + jnp.sum(exp_others, axis=1, keepdims=True)
    probs = (exp_others / partition).astype(jnp.bfloat16)
    own_prob = exp_own / partition

    low, high = probs[:, :256], probs[:, 256:]
    c_send[...] = dot_first(jnp.where(c == 0, high, low), hidden).astype(jnp.bfloat16)
    c_reduce = pltpu.make_async_remote_copy(
        src_ref=c_send, dst_ref=c_recv, send_sem=rc_send.at[0], recv_sem=rc_recv.at[0],
        device_id=sibling, device_id_type=MESH)
    c_reduce.start()
    own_half[...] = dot_first(jnp.where(c == 0, low, high), hidden)
    c_reduce.wait_recv()
    xy_send[...] = (own_half[...] + c_recv[...].astype(jnp.float32)).astype(jnp.bfloat16).reshape(16, 16, WIDTH)
    here = x * 4 + y

    def xy_copy(k):
        there, target = xy_peer(k)
        return pltpu.make_async_remote_copy(
            src_ref=xy_send.at[there], dst_ref=xy_recv.at[here], send_sem=rxy_send.at[k - 1],
            recv_sem=rxy_recv.at[k - 1], device_id=target, device_id_type=MESH)

    def xy_arrived(k):
        part = xy_recv.at[((x + 4 - k // 4) % 4) * 4 + (y + 4 - k % 4) % 4]
        pltpu.make_async_remote_copy(
            src_ref=part, dst_ref=part, send_sem=rxy_send.at[k - 1], recv_sem=rxy_recv.at[k - 1],
            device_id=sibling, device_id_type=MESH).wait_recv()

    for k in range(1, 16):
        xy_copy(k).start()
    xy_recv[here] = xy_send[here]

    d_hidden = (own_prob - 1.0) * positives + dot(probs, negs[...])
    gg_out[...] = (d_hidden * normed).astype(jnp.bfloat16)
    d_normed = d_hidden * gates
    d_att[...] = (
        inverse_rms * (d_normed - normed * jnp.mean(d_normed * normed, axis=1, keepdims=True))
    ).astype(jnp.bfloat16)

    att[...] = jnp.zeros_like(att)

    def back_step(e, carry):
        back, q = rank_of(e)
        hb = h - back
        for head in range(HEADS):
            lanes = pl.ds(head * HEAD, HEAD)
            k_head = kv[hb, q, 0, :, :, :, lanes].reshape(8 * QUARTER, HEAD)
            v_head = kv[hb, q, 1, :, :, :, lanes].reshape(8 * QUARTER, HEAD)
            d_weights = dot_last(d_att[:, lanes], v_head)
            d_scores = (d_weights * slope[e, head]).astype(jnp.bfloat16)
            att[:, lanes] += dot(d_scores, k_head)
        return carry

    lax.fori_loop(0, ranks, back_step, 0)

    for k in range(1, 16):
        xy_arrived(k)
    total = xy_recv[0].astype(jnp.float32)
    for k in range(1, 16):
        total = total + xy_recv[k].astype(jnp.float32)
    for row in range(16):
        for part in range(4):
            z_send[row, part:part + 1, :] = total[row:row + 1, part * 128:(part + 1) * 128]

    def z_copy(k):
        there, target = z_peer(k)
        return pltpu.make_async_remote_copy(
            src_ref=z_send.at[there], dst_ref=z_recv.at[z], send_sem=rz_send.at[k - 1],
            recv_sem=rz_recv.at[k - 1], device_id=target, device_id_type=MESH)

    def z_arrived(k):
        part = z_recv.at[(z + 16 - k) % 16]
        pltpu.make_async_remote_copy(
            src_ref=part, dst_ref=part, send_sem=rz_send.at[k - 1], recv_sem=rz_recv.at[k - 1],
            device_id=sibling, device_id_type=MESH).wait_recv()

    for k in (8, 7, 9, 6, 10, 5, 11, 4, 12, 3, 13, 2, 14, 1, 15):
        z_copy(k).start()
    z_recv[z] = z_send[z]
    gq_out[...] = att[...].astype(jnp.bfloat16)

    for q in range(4):
        pl.when(sends_forward(q))(lambda q=q: forward(h, q, 0).wait_send())
        if q > 0:
            pl.when(sends_backward(q))(lambda q=q: backward(h, q, 0).wait_send())

    @pl.when(x == y)
    def _():
        for k in (1, 2, 3):
            neg_x(k).wait_send()

    for k in (1, 2, 3):
        neg_z(k).wait_send()
        neg_y(k).wait_send()
    neg_c(c).wait_send()

    @pl.when(h == 0)
    def _():
        for q in (1, 2, 3):
            backward(1, q, 1).wait_send()

    @pl.when(h == 3)
    def _():
        for q in (2, 3):
            backward(0, q, 1).wait_send()

    def drain(e, carry):
        back, q = rank_of(e)
        hb = h - back
        pl.when(z_forwards(back, q))(lambda: forward(hb, q, 1).wait_send())
        pl.when(z_backwards(back, q))(lambda: backward(hb, q, 1).wait_send())
        for k in (1, 2, 3):
            y2 = (y + k) % 4
            pl.when(goes_to(back, y2))(lambda k=k: y_copy(e, hb, q, k).wait_send())
            pl.when(comes_from(back, y2))(lambda y2=y2: c_copy(e, hb, q, y2).wait_send())
        c_copy(e, hb, q, y).wait_send()
        return carry

    lax.fori_loop(0, ranks, drain, 0)
    c_reduce.wait_send()
    for k in range(1, 16):
        xy_copy(k).wait_send()

    for k in range(1, 16):
        z_arrived(k)
    grad = z_recv[0]
    for k in range(1, 16):
        grad = grad + z_recv[k]
    for part in range(4):
        gn_out[:, part * 128:(part + 1) * 128] = grad[part:part + 1, :]
    for k in range(1, 16):
        z_copy(k).wait_send()


def on_device(query_rows, key_rows, value_rows, gate_rows, positives, negatives, history_lengths):
    vmem = pl.BlockSpec(memory_space=pltpu.VMEM)
    hbm = pl.BlockSpec(memory_space=pl.ANY)
    smem = pl.BlockSpec(memory_space=pltpu.SMEM)
    dma = pltpu.SemaphoreType.DMA
    bf16, f32 = jnp.bfloat16, jnp.float32
    return pl.pallas_call(
        kernel,
        out_shape=(
            jax.ShapeDtypeStruct((ROWS, WIDTH), bf16),
            jax.ShapeDtypeStruct((ROWS, WIDTH), bf16),
            jax.ShapeDtypeStruct((1, WIDTH), f32),
        ),
        in_specs=[smem, vmem, hbm, hbm, vmem, vmem, vmem],
        out_specs=(vmem, vmem, vmem),
        scratch_shapes=[
            pltpu.VMEM((4, 4, 2, 4, 2, QUARTER, WIDTH), bf16),
            pltpu.VMEM((ROWS, WIDTH), f32),
            pltpu.VMEM((12, HEADS, ROWS, 8 * QUARTER), f32),
            pltpu.VMEM((4, 2, 4, 16, WIDTH), bf16),
            pltpu.VMEM((512, WIDTH), bf16),
            pltpu.VMEM((ROWS, WIDTH), bf16),
            pltpu.VMEM((256, WIDTH), bf16),
            pltpu.VMEM((256, WIDTH), bf16),
            pltpu.VMEM((256, WIDTH), f32),
            pltpu.VMEM((16, 16, WIDTH), bf16),
            pltpu.VMEM((16, 16, WIDTH), bf16),
            pltpu.VMEM((16, 4, 128), f32),
            pltpu.VMEM((16, 4, 128), f32),
            dma((8,)), dma((4, 4, 4, 2)), dma((2, 2, 4)), dma((12, 3)), dma((12, 4)),
            dma((3,)), dma((1,)), dma((3,)), dma((3,)), dma((3,)), dma((3,)), dma((1,)), dma((1,)),
            dma((1,)), dma((1,)), dma((15,)), dma((15,)), dma((15,)), dma((15,)),
        ],
        name="layer",
        compiler_params=pltpu.CompilerParams(
            collective_id=0, has_side_effects=True, vmem_limit_bytes=48 * 2**20),
    )(history_lengths, query_rows, key_rows, value_rows, gate_rows, positives, negatives)


def solution(mesh):
    rows = P(("dp", "ctx"), None)
    return jax.shard_map(
        on_device,
        mesh=mesh,
        in_specs=(rows, rows, rows, rows, rows, P("dp", None), P("dp", None)),
        out_specs=(rows, rows, rows),
        check_vma=False,
    )
```

```python
import jax
import jax.numpy as jnp
from jax import lax
from jax.experimental import pallas as pl
from jax.experimental.pallas import tpu as pltpu
from jax.sharding import PartitionSpec as P

HEADS = 4
HEAD = 128
WIDTH = 512
ROWS = 128
QUARTER = 32
SCALE = HEAD ** (-0.5)
EPS = 1e-05
MESH = pl.DeviceIdType.MESH

ORDER_1 = (0, 1, 2, 3)
ORDER_2 = (0, 2, 4, 6, 5, 7, 3, 1)
ORDER_3 = (0, 1, 5, 4, 2, 6, 3, 7)

FORWARD = (
    ((0, 0), (0, 1), (0, 2), (0, 3), None),
    ((0, 0), (0, 2), (1, 0), (1, 1), (0, 3)),
    ((0, 0), (0, 1), (1, 0), (0, 2), (0, 3)),
    (None,) * 5,
)
BACKWARD = (
    ((0, 2), (0, 3), (-1, 1), (-1, 2), (-1, 3)),
    ((0, 1), (0, 2), (0, 3), None, None),
    (None,) * 5,
    (None, None, (3, 2), (3, 3), (2, 1)),
)


def packed(order):
    return sum(code << (3 * place) for place, code in enumerate(order))


def pick(h, values):
    out = jnp.int32(values[3])
    for index in (2, 1, 0):
        out = jnp.where(h == index, jnp.int32(values[index]), out)
    return out


def dot_last(a, b):
    return lax.dot_general(a, b, (((1,), (1,)), ((), ())), preferred_element_type=jnp.float32)


def dot_first(a, b):
    return lax.dot_general(a, b, (((0,), (0,)), ((), ())), preferred_element_type=jnp.float32)


def dot(a, b):
    return jnp.dot(a, b, preferred_element_type=jnp.float32)


def kernel(
    lengths_hbm, q_hbm, k_hbm, v_hbm, gate_hbm, pos_hbm, neg_hbm,
    gq_out, gg_out, gn_out,
    lengths, q_ref, gate_ref, pos_ref, neg_ref, kv, att, slope, negs_raw, negs, d_att, c_send, c_recv, own_half, xy_send, xy_recv, z_send, z_recv,
    ready_x, ready_z, local_sem, kv_recv, z_sem, y_sem, c_sem,
    nx_send, nx_recv, nl_send, nl_recv, ny_send, ny_recv, nc_send, nc_recv,
    rc_send, rc_recv, rxy_send, rxy_recv, rz_send, rz_recv,
):
    dp, ctx = lax.axis_index("dp"), lax.axis_index("ctx")
    x, l = dp // 4, dp % 4
    h, y, c = ctx // 8, (ctx // 2) % 4, ctx % 2
    z = h * 4 + l

    def device(x2, l2, h2, y2, c2):
        return (x2 * 4 + l2, (h2 * 4 + y2) * 2 + c2)

    sibling = device(x, l, h, y, 1 - c)

    def z_peer(k):
        z2 = (z + k) % 16
        return z2, device(x, z2 % 4, z2 // 4, y, c)

    def xy_peer(k):
        x2, y2 = (x + k // 4) % 4, (y + k % 4) % 4
        return x2 * 4 + y2, device(x2, l, h, y2, c)

    local = []
    for q in range(4):
        for kind, source in ((0, k_hbm), (1, v_hbm)):
            local.append(pltpu.make_async_copy(
                source.at[pl.ds(q * QUARTER, QUARTER)], kv.at[h, q, kind, y, c], local_sem.at[q * 2 + kind]))
    others = []
    for source, target in (
        (lengths_hbm, lengths), (neg_hbm, neg_ref), (q_hbm, q_ref), (gate_hbm, gate_ref), (pos_hbm, pos_ref)
    ):
        others.append(pltpu.make_async_copy(source, target, local_sem.at[8 + len(others)]))
    for copy in local + others:
        copy.start()

    barrier = pltpu.get_barrier_semaphore()
    pl.semaphore_signal(barrier, inc=1, device_id=sibling, device_id_type=MESH)
    for k in (1, 2, 4, 12, 14, 15):
        pl.semaphore_signal(barrier, inc=1, device_id=z_peer(k)[1], device_id_type=MESH)
    for k in (1, 2, 3, 4, 8, 12):
        pl.semaphore_signal(barrier, inc=1, device_id=xy_peer(k)[1], device_id_type=MESH)

    for y2 in range(4):
        @pl.when(y2 > y)
        def _():
            for q in range(4):
                kv[h, q, :, y2] = jnp.zeros((2, 2, QUARTER, WIDTH), jnp.bfloat16)

        @pl.when((h >= 2) & (y2 < y))
        def _():
            for q in range(4):
                kv[h - 2, q, :, y2] = jnp.zeros((2, 2, QUARTER, WIDTH), jnp.bfloat16)

    att[...] = jnp.zeros_like(att)
    for copy in local:
        copy.wait()
    pl.semaphore_wait(barrier, 13)

    def piece_copy(hb, q, y2, c2, send_sem, target):
        piece = kv.at[hb, q, :, y2, c2]
        return pltpu.make_async_remote_copy(
            src_ref=piece, dst_ref=piece, send_sem=send_sem, recv_sem=kv_recv.at[hb, q, y2, c2],
            device_id=target, device_id_type=MESH)

    def piece_arrived(hb, q, y2, c2):
        piece_copy(hb, q, y2, c2, z_sem.at[0, 0], sibling).wait_recv()

    def z_copy_of(way, number, hh, back, q):
        target = device(x, l, (hh + (1 if way == 0 else 3)) % 4, y, c)
        return piece_copy(hh - back, q, y, c, z_sem.at[way, number], target)

    def z_round(number):
        for way, table in ((0, FORWARD), (1, BACKWARD)):
            for hh in range(4):
                @pl.when(h == hh)
                def _():
                    earlier = [n for n in range(number) if table[hh][n] is not None]
                    if table[hh][number] is not None:
                        back, q = table[hh][number]
                        if earlier:
                            z_copy_of(way, earlier[-1], hh, *table[hh][earlier[-1]]).wait_send()
                        if back in (-1, 3):
                            piece_arrived(hh - back, q, y, c)
                        z_copy_of(way, number, hh, back, q).start()

    def z_rounds_left():
        for way, table in ((0, FORWARD), (1, BACKWARD)):
            for hh in range(4):
                used = [n for n in range(5) if table[hh][n] is not None]
                if used:
                    last = z_copy_of(way, used[-1], hh, *table[hh][used[-1]])
                    pl.when(h == hh)(lambda last=last: last.wait_send())

    z_round(0)

    for k in (4, 8, 12):
        pl.semaphore_signal(ready_x, inc=1, device_id=xy_peer(k)[1], device_id_type=MESH)
    for k in (4, 12):
        pl.semaphore_signal(ready_z.at[0], inc=1, device_id=z_peer(k)[1], device_id_type=MESH)

    def neg_x(k):
        part = neg_ref.at[pl.ds(c * 16, 16)]
        return pltpu.make_async_remote_copy(
            src_ref=part, dst_ref=negs_raw.at[y, c, l], send_sem=nx_send.at[k - 1], recv_sem=nx_recv.at[0],
            device_id=device((x + k) % 4, l, h, y, c), device_id_type=MESH)

    def neg_z(k):
        part = negs_raw.at[y, c, l]
        l2 = (l + k) % 4
        z2 = (z + (k if k < 3 else 15)) % 16
        return pltpu.make_async_remote_copy(
            src_ref=part, dst_ref=part, send_sem=nl_send.at[k - 1], recv_sem=nl_recv.at[k - 1],
            device_id=device(x, l2, z2 // 4, y, c), device_id_type=MESH)

    def neg_z_arrived(k):
        part = negs_raw.at[y, c, (l + 4 - k) % 4]
        pltpu.make_async_remote_copy(
            src_ref=part, dst_ref=part, send_sem=nl_send.at[k - 1], recv_sem=nl_recv.at[k - 1],
            device_id=sibling, device_id_type=MESH).wait_recv()

    def neg_y(k):
        part = negs_raw.at[y, c]
        return pltpu.make_async_remote_copy(
            src_ref=part, dst_ref=part, send_sem=ny_send.at[k - 1], recv_sem=ny_recv.at[k - 1],
            device_id=device(x, l, h, (y + k) % 4, c), device_id_type=MESH)

    def neg_y_arrived(k):
        part = negs_raw.at[(y + 4 - k) % 4, c]
        pltpu.make_async_remote_copy(
            src_ref=part, dst_ref=part, send_sem=ny_send.at[k - 1], recv_sem=ny_recv.at[k - 1],
            device_id=sibling, device_id_type=MESH).wait_recv()

    def neg_c(c2):
        part = negs_raw.at[:, c2]
        return pltpu.make_async_remote_copy(
            src_ref=part, dst_ref=part, send_sem=nc_send.at[0], recv_sem=nc_recv.at[0],
            device_id=sibling, device_id_type=MESH)

    for copy in others:
        copy.wait()

    @pl.when(x == y)
    def _():
        for k in (1, 2, 3):
            neg_x(k).start()

    places = ctx * ROWS + lax.broadcasted_iota(jnp.int32, (ROWS, 1), 0)
    first = jnp.zeros((ROWS, 1), jnp.int32)
    user_end = jnp.int32(0)
    for user in range(4):
        user_end = user_end + lengths[0, user]
        first = jnp.where(places >= user_end, user_end, first)

    orders = pick(h, [0, packed(ORDER_1), packed(ORDER_2), packed(ORDER_3)])
    ranks = pick(h, [4, 8, 12, 12])

    def rank_of(e):
        code = lax.shift_right_logical(orders, 3 * jnp.maximum(e - 4, 0)) & 7
        back = jnp.where(e < 4, 0, 1 + code // 4)
        return back, jnp.where(e < 4, e, code % 4)

    def comes_from(back, y2):
        return (back == 1) | ((back == 0) & (y2 < y)) | ((back == 2) & (y2 > y))

    def goes_to(back, y2):
        return (back == 1) | ((back == 0) & (y2 > y)) | ((back == 2) & (y2 < y))

    def y_copy(e, hb, q, k):
        return piece_copy(hb, q, y, c, y_sem.at[e, k - 1], device(x, l, h, (y + k) % 4, c))

    def c_copy(e, hb, q, y2):
        return piece_copy(hb, q, y2, c, c_sem.at[e, y2], sibling)

    def column_event(e):
        back, q = rank_of(e)
        hb = h - back
        pl.when(back > 0)(lambda: piece_arrived(hb, q, y, c))
        for k in (1, 3, 2):
            pl.when(goes_to(back, (y + k) % 4))(lambda k=k: y_copy(e, hb, q, k).start())
        c_copy(e, hb, q, y).start()

    def row_event(e):
        back, q = rank_of(e)
        hb = h - back
        for k in (1, 3, 2):
            y2 = (y + k) % 4

            @pl.when(comes_from(back, y2))
            def _():
                piece_arrived(hb, q, y2, c)
                c_copy(e, hb, q, y2).start()

    def compute_event(e):
        back, q = rank_of(e)
        hb = h - back
        for k in range(4):
            y2 = (y + k) % 4
            pl.when(True if k == 0 else comes_from(back, y2))(lambda y2=y2: piece_arrived(hb, q, y2, 1 - c))
        at = lax.broadcasted_iota(jnp.int32, (ROWS, 8 * QUARTER), 1)
        k_places = hb * 1024 + q * QUARTER + (at // QUARTER) * ROWS + at % QUARTER
        allowed = (k_places >= first) & (k_places <= places)
        for head in range(HEADS):
            lanes = pl.ds(head * HEAD, HEAD)
            k_head = kv[hb, q, 0, :, :, :, lanes].reshape(8 * QUARTER, HEAD)
            v_head = kv[hb, q, 1, :, :, :, lanes].reshape(8 * QUARTER, HEAD)
            logits = dot_last(q_ref[:, lanes], k_head)
            sigmoid = 0.5 * jnp.tanh(logits * (0.5 * SCALE)) + 0.5
            silu = logits * SCALE * sigmoid
            weights = jnp.where(allowed, silu, 0.0).astype(jnp.bfloat16)
            slope[e, head] = jnp.where(allowed, (sigmoid + silu * (1.0 - sigmoid)) * SCALE, 0.0)
            att[:, lanes] += dot(weights, v_head)

    def step(e, carry):
        pl.when((e >= 4) & (e < ranks))(lambda: column_event(e))
        pl.when(e == 3)(lambda: z_round(1))

        @pl.when(h != 0)
        def _():
            for number in (2, 3, 4):
                pl.when(e == number + 2)(lambda number=number: z_round(number))

        @pl.when(e == 2)
        def _():
            @pl.when(x != y)
            def _():
                part = negs_raw.at[y, c, l]
                pltpu.make_async_remote_copy(
                    src_ref=part, dst_ref=part, send_sem=nx_send.at[0], recv_sem=nx_recv.at[0],
                    device_id=sibling, device_id_type=MESH).wait_recv()

            @pl.when(x == y)
            def _():
                negs_raw[y, c, l] = neg_ref[pl.ds(pl.multiple_of(c * 16, 16), 16), :]

            for k in (1, 2, 3):
                neg_z(k).start()

        @pl.when(e == 4)
        def _():
            pl.semaphore_wait(ready_z.at[0], 2)
            for k in (4, 12):
                pl.semaphore_signal(ready_z.at[1], inc=1, device_id=z_peer(k)[1], device_id_type=MESH)
            for k in (1, 2, 3):
                neg_z_arrived(k)
            for k in (1, 2, 3):
                neg_y(k).start()

        @pl.when(e == 5)
        def _():
            for k in (1, 2, 3):
                neg_y_arrived(k)
            neg_c(c).start()

        pl.when(e >= 2)(lambda: compute_event(e - 2))
        pl.when((e >= 1) & (e <= ranks))(lambda: row_event(e - 1))
        return carry

    for e in range(4):
        column_event(e)
    lax.fori_loop(0, ranks + 2, step, 0)

    @pl.when(h == 0)
    def _():
        for number in (2, 3, 4):
            z_round(number)

    neg_c(1 - c).wait_recv()
    to = lax.broadcasted_iota(jnp.int32, (512, 512), 0)
    source = ((((to // 64) % 4 * 2 + (to // 8) % 2) * 4 + to % 4) * 16
              + (to // 4) % 2 * 8 + (to // 16) % 4 * 2 + to // 256)
    chosen = lax.broadcasted_iota(jnp.int32, (512, 512), 1) == source
    negs[...] = dot(
        jnp.where(chosen, 1.0, 0.0).astype(jnp.bfloat16), negs_raw[...].reshape(512, WIDTH)
    ).astype(jnp.bfloat16)

    attended = att[...]
    inverse_rms = lax.rsqrt(jnp.mean(attended * attended, axis=1, keepdims=True) + EPS)
    normed = attended * inverse_rms
    gates = gate_ref[...].astype(jnp.float32)
    positives = pos_ref[...].astype(jnp.float32)
    hidden = (normed * gates).astype(jnp.bfloat16)
    own_logit = jnp.sum(hidden.astype(jnp.float32) * positives, axis=1, keepdims=True)
    other_logits = dot_last(hidden, negs[...])
    largest = jnp.maximum(own_logit, jnp.max(other_logits, axis=1, keepdims=True))
    exp_own = jnp.exp(own_logit - largest)
    exp_others = jnp.exp(other_logits - largest)
    partition = exp_own + jnp.sum(exp_others, axis=1, keepdims=True)
    probs = (exp_others / partition).astype(jnp.bfloat16)
    own_prob = exp_own / partition

    low, high = probs[:, :256], probs[:, 256:]
    c_send[...] = dot_first(jnp.where(c == 0, high, low), hidden).astype(jnp.bfloat16)
    c_reduce = pltpu.make_async_remote_copy(
        src_ref=c_send, dst_ref=c_recv, send_sem=rc_send.at[0], recv_sem=rc_recv.at[0],
        device_id=sibling, device_id_type=MESH)
    c_reduce.start()
    own_half[...] = dot_first(jnp.where(c == 0, low, high), hidden)
    c_reduce.wait_recv()
    xy_send[...] = (own_half[...] + c_recv[...].astype(jnp.float32)).astype(jnp.bfloat16).reshape(16, 16, WIDTH)
    here = x * 4 + y

    def xy_copy(k):
        there, target = xy_peer(k)
        return pltpu.make_async_remote_copy(
            src_ref=xy_send.at[there], dst_ref=xy_recv.at[here], send_sem=rxy_send.at[k - 1],
            recv_sem=rxy_recv.at[k - 1], device_id=target, device_id_type=MESH)

    def xy_arrived(k):
        part = xy_recv.at[((x + 4 - k // 4) % 4) * 4 + (y + 4 - k % 4) % 4]
        pltpu.make_async_remote_copy(
            src_ref=part, dst_ref=part, send_sem=rxy_send.at[k - 1], recv_sem=rxy_recv.at[k - 1],
            device_id=sibling, device_id_type=MESH).wait_recv()

    pl.semaphore_wait(ready_x, 3)
    for k in range(1, 16):
        xy_copy(k).start()
    xy_recv[here] = xy_send[here]

    d_hidden = (own_prob - 1.0) * positives + dot(probs, negs[...])
    gg_out[...] = (d_hidden * normed).astype(jnp.bfloat16)
    d_normed = d_hidden * gates
    d_att[...] = (
        inverse_rms * (d_normed - normed * jnp.mean(d_normed * normed, axis=1, keepdims=True))
    ).astype(jnp.bfloat16)

    att[...] = jnp.zeros_like(att)

    def back_step(e, carry):
        back, q = rank_of(e)
        hb = h - back
        for head in range(HEADS):
            lanes = pl.ds(head * HEAD, HEAD)
            k_head = kv[hb, q, 0, :, :, :, lanes].reshape(8 * QUARTER, HEAD)
            v_head = kv[hb, q, 1, :, :, :, lanes].reshape(8 * QUARTER, HEAD)
            d_weights = dot_last(d_att[:, lanes], v_head)
            d_scores = (d_weights * slope[e, head]).astype(jnp.bfloat16)
            att[:, lanes] += dot(d_scores, k_head)
        return carry

    lax.fori_loop(0, ranks, back_step, 0)

    for k in range(1, 16):
        xy_arrived(k)
    total = xy_recv[0].astype(jnp.float32)
    for k in range(1, 16):
        total = total + xy_recv[k].astype(jnp.float32)
    for row in range(16):
        for part in range(4):
            z_send[row, part:part + 1, :] = total[row:row + 1, part * 128:(part + 1) * 128]

    def z_copy(k):
        there, target = z_peer(k)
        return pltpu.make_async_remote_copy(
            src_ref=z_send.at[there], dst_ref=z_recv.at[z], send_sem=rz_send.at[k - 1],
            recv_sem=rz_recv.at[k - 1], device_id=target, device_id_type=MESH)

    def z_arrived(k):
        part = z_recv.at[(z + 16 - k) % 16]
        pltpu.make_async_remote_copy(
            src_ref=part, dst_ref=part, send_sem=rz_send.at[k - 1], recv_sem=rz_recv.at[k - 1],
            device_id=sibling, device_id_type=MESH).wait_recv()

    pl.semaphore_wait(ready_z.at[1], 2)
    for k in (8, 7, 9, 6, 10, 5, 11, 4, 12, 3, 13, 2, 14, 1, 15):
        z_copy(k).start()
    z_recv[z] = z_send[z]
    gq_out[...] = att[...].astype(jnp.bfloat16)

    z_rounds_left()

    @pl.when(x == y)
    def _():
        for k in (1, 2, 3):
            neg_x(k).wait_send()

    for k in (1, 2, 3):
        neg_z(k).wait_send()
        neg_y(k).wait_send()
    neg_c(c).wait_send()

    def drain(e, carry):
        back, q = rank_of(e)
        hb = h - back
        for k in (1, 2, 3):
            y2 = (y + k) % 4
            pl.when(goes_to(back, y2))(lambda k=k: y_copy(e, hb, q, k).wait_send())
            pl.when(comes_from(back, y2))(lambda y2=y2: c_copy(e, hb, q, y2).wait_send())
        c_copy(e, hb, q, y).wait_send()
        return carry

    lax.fori_loop(0, ranks, drain, 0)
    c_reduce.wait_send()
    for k in range(1, 16):
        xy_copy(k).wait_send()

    for k in range(1, 16):
        z_arrived(k)
    grad = z_recv[0]
    for k in range(1, 16):
        grad = grad + z_recv[k]
    for part in range(4):
        gn_out[:, part * 128:(part + 1) * 128] = grad[part:part + 1, :]
    for k in range(1, 16):
        z_copy(k).wait_send()


def on_device(query_rows, key_rows, value_rows, gate_rows, positives, negatives, history_lengths):
    vmem = pl.BlockSpec(memory_space=pltpu.VMEM)
    hbm = pl.BlockSpec(memory_space=pltpu.HBM)
    dma = pltpu.SemaphoreType.DMA
    bf16, f32 = jnp.bfloat16, jnp.float32
    return pl.pallas_call(
        kernel,
        out_shape=(
            jax.ShapeDtypeStruct((ROWS, WIDTH), bf16),
            jax.ShapeDtypeStruct((ROWS, WIDTH), bf16),
            jax.ShapeDtypeStruct((1, WIDTH), f32),
        ),
        in_specs=[hbm] * 7,
        out_specs=(vmem, vmem, vmem),
        scratch_shapes=[
            pltpu.SMEM((1, 4), jnp.int32),
            pltpu.VMEM((ROWS, WIDTH), bf16),
            pltpu.VMEM((ROWS, WIDTH), bf16),
            pltpu.VMEM((ROWS, WIDTH), bf16),
            pltpu.VMEM((32, WIDTH), bf16),
            pltpu.VMEM((4, 4, 2, 4, 2, QUARTER, WIDTH), bf16),
            pltpu.VMEM((ROWS, WIDTH), f32),
            pltpu.VMEM((12, HEADS, ROWS, 8 * QUARTER), f32),
            pltpu.VMEM((4, 2, 4, 16, WIDTH), bf16),
            pltpu.VMEM((512, WIDTH), bf16),
            pltpu.VMEM((ROWS, WIDTH), bf16),
            pltpu.VMEM((256, WIDTH), bf16),
            pltpu.VMEM((256, WIDTH), bf16),
            pltpu.VMEM((256, WIDTH), f32),
            pltpu.VMEM((16, 16, WIDTH), bf16),
            pltpu.VMEM((16, 16, WIDTH), bf16),
            pltpu.VMEM((16, 4, 128), f32),
            pltpu.VMEM((16, 4, 128), f32),
            pltpu.SemaphoreType.REGULAR, pltpu.SemaphoreType.REGULAR((2,)),
            dma((13,)), dma((4, 4, 4, 2)), dma((2, 5)), dma((12, 3)), dma((12, 4)),
            dma((3,)), dma((1,)), dma((3,)), dma((3,)), dma((3,)), dma((3,)), dma((1,)), dma((1,)),
            dma((1,)), dma((1,)), dma((15,)), dma((15,)), dma((15,)), dma((15,)),
        ],
        name="layer",
        compiler_params=pltpu.CompilerParams(
            collective_id=0, has_side_effects=True, vmem_limit_bytes=64 * 2**20),
    )(history_lengths, query_rows, key_rows, value_rows, gate_rows, positives, negatives)

def solution(mesh):
    rows = P(("dp", "ctx"), None)
    return jax.shard_map(
        on_device,
        mesh=mesh,
        in_specs=(rows, rows, rows, rows, rows, P("dp", None), P("dp", None)),
        out_specs=(rows, rows, rows),
        check_vma=False,
    )
```
